512 devices in a mesh: row: 16 (over z), col: 32 (over x, y, core).
Axes of the slice: x: 4, y: 4, z: 16, core: 2. Of those that a mesh axis runs over, the one named last changes fastest.
Arguments:
- band: float32 [2, 512, 65536], P(None, 'row', 'col'), may hold values from -6 to 6
- sources: int32 [512, 4], P('row'), may hold values from 0 to 511, as said below
- taps: float32 [512, 4], P('row'), may hold values from 0.1 to 1
- jacobian: float32 [512, 65536], P('row', 'col'), may hold values from 0.3 to 3
- phase: float32 [512, 65536], P('row', 'col'), may hold values from -3.140625 to 3.140625
Outputs:
- tilted: float32 [2, 512, 65536], P(None, 'row', 'col')
The draws below stay inside these ranges and needn't reach their ends.
Inputs may be any that keep to these rules, and one draw needn't show every extreme that they name: Row r's sources are four consecutive rows b, b + 1, b + 2, b + 3 with r - 16 <= b and b + 3 <= r + 16.
All inputs are finite; a program needn't handle non-finite values.
Results may differ from the reference program's by a relative error of at most 0.00007.
Values sent between devices are 32-bit elements; how exact they have to be, the bound alone decides.
No kernel may reach another device: no remote copies, remote signals or barrier semaphores. Data moves between devices by JAX's collectives and lax.ppermute only.
A program may use at most 192 MiB of HBM per device.

```python
import math
import jax
import jax.numpy as jnp

W = 65536
ROWS_DEV = 32
HALO = 16
NR = 512


def draw_sources(key, part):
    key = jax.random.fold_in(key, 7)
    rows = jnp.arange(NR, dtype=jnp.int32)
    offset = jax.random.randint(key, (NR,), -HALO, HALO - 2, dtype=jnp.int32)
    within = rows % ROWS_DEV
    offset = jnp.where(within == 0, -HALO, offset)
    offset = jnp.where(within == ROWS_DEV - 1, HALO - 3, offset)
    base = jnp.clip(rows + offset, 0, NR - 4)
    return (base[:, None] + jnp.arange(4, dtype=jnp.int32)[None, :]).astype(jnp.int32)


def steps_of(own_key, shape, shards, smallest, largest):
    factor_of = 1.0
    for position, blocks in shards:
        draws = jax.random.uniform(jax.random.fold_in(jax.random.fold_in(own_key, 6), position), (blocks,), jnp.float32, smallest / len(shards), largest / len(shards))
        factor_of = factor_of * jnp.repeat(jnp.exp(draws), shape[position] // blocks).reshape((-1,) + (1,) * (len(shape) - 1 - position))
    return factor_of


def noise(key, shape, deviation, reach, split=(), kind=jnp.bfloat16):
    entries = deviation * jax.random.normal(key, shape, jnp.float32)
    if split:
        entries = entries * steps_of(key, shape, split, -0.22, 0.18)
    return jnp.clip(entries, -reach, reach).astype(kind)


def setup_inputs(seed: int = 0) -> dict:
    seeds = jax.random.split(jax.random.key(seed), 6)
    band = noise(seeds[0], (2, NR, W), 1.0, 6.0, ((1, 16), (2, 32)), jnp.float32)
    sources = draw_sources(jax.random.fold_in(seeds[5], 71), 0)
    taps = jnp.clip(0.1 + 0.9 * jax.random.uniform(seeds[2], (NR, 4), jnp.float32) ** steps_of(seeds[2], (NR, 4), ((0, 16),), -0.2, 0.2), 0.1, 1.0)
    jacobian = jnp.clip(jnp.exp(math.log(3.0) - 2.3025851 * jax.random.uniform(seeds[3], (NR, W), jnp.float32) ** steps_of(seeds[3], (NR, W), ((0, 16), (1, 32)), -0.2, 0.2)), 0.3, 3.0)
    phase = jnp.clip(jax.random.uniform(seeds[4], (NR, W), jnp.float32, -3.140625, 3.140625), -3.140625, 3.140625)
    return dict(band=band, sources=sources, taps=taps, jacobian=jacobian, phase=phase)


def reference(band, sources, taps, jacobian, phase):
    field = band[0] + 1j * band[1]
    spectrum = jnp.fft.fft(field, axis=-1)
    scale = 1.0 / jnp.sqrt(jnp.float32(W))
    spec_re = jnp.real(spectrum).astype(band.dtype) * scale
    spec_im = jnp.imag(spectrum).astype(band.dtype) * scale
    acc_re = jnp.zeros_like(spec_re)
    acc_im = jnp.zeros_like(spec_im)
    for j in range(4):
        index = sources[:, j].astype(jnp.int32)
        weight = taps[:, j][:, None]
        acc_re = acc_re + weight * jnp.take(spec_re, index, axis=0)
        acc_im = acc_im + weight * jnp.take(spec_im, index, axis=0)
    cosine = jnp.cos(phase)
    sine = jnp.sin(phase)
    out_re = jacobian * (acc_re * cosine - acc_im * sine)
    out_im = jacobian * (acc_re * sine + acc_im * cosine)
    return jnp.stack([out_re, out_im])
```

```python
import math

import jax
import jax.numpy as jnp
import numpy as np
from jax import lax
from jax.experimental import pallas as pl
from jax.experimental.pallas import tpu as pltpu
from jax.sharding import PartitionSpec as P

N1 = 256
LANES = 128
ROWS = 32
HALO = 16
TILES = 16
SLAB = 32


def split_bf16(x):
    hi = x.astype(jnp.bfloat16)
    lo = (x - hi.astype(jnp.float32)).astype(jnp.bfloat16)
    return hi, lo


def dft_tables():
    idx = np.arange(N1, dtype=np.int64)
    ang = 2.0 * np.pi * ((idx[:, None] * idx[None, :]) % N1) / N1
    cos, sin = np.cos(ang), np.sin(ang)
    table = np.block([[cos, sin], [-sin, cos]])
    hi = table.astype(np.float32).astype(jnp.bfloat16)
    lo = (table - hi.astype(np.float64)).astype(np.float32).astype(jnp.bfloat16)
    twist = -2.0 * np.pi * (idx[:, None] * idx[None, :]) / (N1 * N1)
    scale = 1.0 / N1
    turn = np.stack([np.cos(twist) * scale, np.sin(twist) * scale]).astype(np.float32)
    return hi, lo, turn


def sine_cosine_coefficients():
    nodes = np.cos((np.arange(400) + 0.5) * np.pi / 400) * (np.pi / 2)
    square = nodes * nodes
    sinc = np.where(nodes == 0, 1.0, np.sin(nodes) / nodes)
    powers = np.stack([square**i for i in range(7)], axis=1)
    sine = np.linalg.lstsq(powers, sinc, rcond=None)[0]
    cosine = np.linalg.lstsq(powers, np.cos(nodes), rcond=None)[0]
    return [float(v) for v in sine], [float(v) for v in cosine]


SINE, COSINE = sine_cosine_coefficients()


def polynomial(square, coefficients):
    total = jnp.full_like(square, coefficients[-1])
    for value in coefficients[-2::-1]:
        total = total * square + value
    return total


def sine_cosine(x):
    half = 0.5 * x
    square = half * half
    s = half * polynomial(square, SINE)
    c = polynomial(square, COSINE)
    return 2.0 * s * c, 1.0 - 2.0 * s * s


def slab_kernel(band_ref, out_ref):
    for c in range(2):
        for tile in range(TILES):
            start = c * 16 + (tile % 2) * 8 + tile // 2
            out_ref[pl.ds(start, ROWS, stride=SLAB), :] = band_ref[
                c, :, tile * LANES : (tile + 1) * LANES
            ]


def transform_kernel(in_ref, hi_ref, lo_ref, turn_ref, out_ref):
    def part(c):
        halves = [in_ref[:, c, h].reshape(N1, LANES) for h in range(2)]
        return jnp.concatenate(halves, axis=1)

    def dot(a, b, contract):
        return lax.dot_general(
            a, b, (((1,), (contract,)), ((), ())), preferred_element_type=jnp.float32
        )

    table_hi, table_lo = hi_ref[...], lo_ref[...]
    field_hi, field_lo = split_bf16(jnp.concatenate([part(0), part(1)], axis=0))
    first = dot(table_hi, field_hi, 0) + (
        dot(table_hi, field_lo, 0) + dot(table_lo, field_hi, 0)
    )
    re, im = first[:N1], first[N1:]
    turn_re, turn_im = turn_ref[0], turn_ref[1]
    turned = jnp.concatenate(
        [re * turn_re - im * turn_im, re * turn_im + im * turn_re], axis=1
    )
    turned_hi, turned_lo = split_bf16(turned)
    final = dot(table_hi, turned_hi, 1) + (
        dot(table_hi, turned_lo, 1) + dot(table_lo, turned_hi, 1)
    )
    for c in range(2):
        for h in range(2):
            out_ref[:, c, h] = final[
                c * N1 : (c + 1) * N1, h * LANES : (h + 1) * LANES
            ].reshape(ROWS, 8, LANES)


def tilt_kernel(base_ref, taps_ref, low_ref, own_ref, high_ref, jac_ref, phase_ref, out_ref, ext, total, sems):
    copies = [
        pltpu.make_async_copy(low_ref, ext.at[0:HALO], sems.at[0]),
        pltpu.make_async_copy(own_ref, ext.at[HALO : HALO + ROWS], sems.at[1]),
        pltpu.make_async_copy(high_ref, ext.at[HALO + ROWS :], sems.at[2]),
    ]
    for copy in copies:
        copy.start()
    for copy in copies:
        copy.wait()
    for r in range(ROWS):
        base = base_ref[r]
        acc = taps_ref[r, 0] * ext[base]
        for j in range(1, 4):
            acc = acc + taps_ref[r, j] * ext[base + j]
        total[r * SLAB : (r + 1) * SLAB, :] = acc
    for tile in range(TILES):
        start = (tile % 2) * 8 + tile // 2
        columns = slice(tile * LANES, (tile + 1) * LANES)
        re = total[pl.ds(start, ROWS, stride=SLAB), :]
        im = total[pl.ds(16 + start, ROWS, stride=SLAB), :]
        sine, cosine = sine_cosine(phase_ref[:, columns])
        jac = jac_ref[:, columns]
        out_ref[0, :, columns] = jac * (re * cosine - im * sine)
        out_ref[1, :, columns] = jac * (re * sine + im * cosine)


def neighbours(value):
    size = lax.axis_size("row")
    up = [(i, i + 1) for i in range(size - 1)]
    down = [(i + 1, i) for i in range(size - 1)]
    low = lax.ppermute(value[ROWS - HALO :], "row", up)
    high = lax.ppermute(value[:HALO], "row", down)
    return low, high


def shards(band, sources, taps, jacobian, phase):
    hi, lo, turn = dft_tables()
    f32 = jnp.float32
    slabs = pl.pallas_call(
        slab_kernel,
        out_shape=jax.ShapeDtypeStruct((ROWS * SLAB, LANES), f32),
        name="slabs",
    )(band)
    rows = lax.all_to_all(
        slabs.reshape(ROWS, 2, 2, 8, LANES), "col", split_axis=0, concat_axis=0, tiled=True
    )
    spectra = pl.pallas_call(
        transform_kernel,
        out_shape=jax.ShapeDtypeStruct((ROWS, 2, 2, 8, LANES), f32),
        name="transform",
        compiler_params=pltpu.CompilerParams(vmem_limit_bytes=24 * 2**20),
    )(rows, jnp.asarray(hi), jnp.asarray(lo), jnp.asarray(turn))
    own = lax.all_to_all(spectra, "col", split_axis=0, concat_axis=0, tiled=True)
    own = own.reshape(ROWS, SLAB, LANES)
    low, high = neighbours(own)
    base = sources[:, 0] - lax.axis_index("row") * ROWS + HALO
    vmem = pl.BlockSpec(memory_space=pltpu.VMEM)
    smem = pl.BlockSpec(memory_space=pltpu.SMEM)
    anywhere = pl.BlockSpec(memory_space=pl.ANY)
    return pl.pallas_call(
        tilt_kernel,
        out_shape=jax.ShapeDtypeStruct(band.shape, f32),
        in_specs=[smem, smem, anywhere, anywhere, anywhere, vmem, vmem],
        out_specs=vmem,
        scratch_shapes=[
            pltpu.VMEM((ROWS + 2 * HALO, SLAB, LANES), f32),
            pltpu.VMEM((ROWS * SLAB, LANES), f32),
            pltpu.SemaphoreType.DMA((3,)),
        ],
        name="tilt",
        compiler_params=pltpu.CompilerParams(vmem_limit_bytes=24 * 2**20),
    )(base, taps, low, own, high, jacobian, phase)


def solution(mesh):
    placed = (
        P(None, "row", "col"),
        P("row", None),
        P("row", None),
        P("row", "col"),
        P("row", "col"),
    )
    return jax.shard_map(
        shards, mesh=mesh, in_specs=placed, out_specs=P(None, "row", "col"), check_vma=False
    )
```

```python
import math

import jax
import jax.numpy as jnp
import numpy as np
from jax import lax
from jax.experimental import pallas as pl
from jax.experimental.pallas import tpu as pltpu
from jax.sharding import PartitionSpec as P

N1 = 256
LANES = 128
ROWS = 32
HALO = 16
TILES = 16
GROUPS = 4
SLAB = 32


def split_bf16(x):
    hi = x.astype(jnp.bfloat16)
    lo = (x - hi.astype(jnp.float32)).astype(jnp.bfloat16)
    return hi, lo


def dft_tables():
    idx = np.arange(N1, dtype=np.int64)
    ang = 2.0 * np.pi * ((idx[:, None] * idx[None, :]) % N1) / N1
    table = np.concatenate([np.cos(ang), np.sin(ang)], axis=1)
    hi = table.astype(np.float32).astype(jnp.bfloat16)
    lo = (table - hi.astype(np.float64)).astype(np.float32).astype(jnp.bfloat16)
    twist = -2.0 * np.pi * (idx[:, None] * idx[None, :]) / (N1 * N1)
    scale = 1.0 / N1
    turn = np.stack([np.cos(twist) * scale, np.sin(twist) * scale]).astype(np.float32)
    return hi, lo, turn


def sine_cosine_coefficients():
    nodes = np.cos((np.arange(400) + 0.5) * np.pi / 400) * (np.pi / 2)
    square = nodes * nodes
    sinc = np.where(nodes == 0, 1.0, np.sin(nodes) / nodes)
    powers = np.stack([square**i for i in range(7)], axis=1)
    sine = np.linalg.lstsq(powers, sinc, rcond=None)[0]
    cosine = np.linalg.lstsq(powers, np.cos(nodes), rcond=None)[0]
    return [float(v) for v in sine], [float(v) for v in cosine]


SINE, COSINE = sine_cosine_coefficients()


def polynomial(square, coefficients):
    total = jnp.full_like(square, coefficients[-1])
    for value in coefficients[-2::-1]:
        total = total * square + value
    return total


def sine_cosine(x):
    half = 0.5 * x
    square = half * half
    s = half * polynomial(square, SINE)
    c = polynomial(square, COSINE)
    return 2.0 * s * c, 1.0 - 2.0 * s * s


def tile_start(tile):
    return (tile % 2) * 8 + tile // 2


def slab_kernel(band_ref, out_ref):
    for group in range(GROUPS):
        rows = slice(8 * group, 8 * group + 8)
        for c in range(2):
            for tile in range(TILES):
                start = 8 * group * SLAB + c * 16 + tile_start(tile)
                out_ref[pl.ds(start, 8, stride=SLAB), :] = band_ref[
                    c, rows, tile * LANES : (tile + 1) * LANES
                ]


def transform_kernel(in_ref, hi_ref, lo_ref, turn_ref, out_ref):
    def part(c):
        halves = [in_ref[:, c, h].reshape(N1, LANES) for h in range(2)]
        return jnp.concatenate(halves, axis=1)

    def blocks(re, im):
        upper = jnp.concatenate([re, im], axis=1)
        return jnp.concatenate([upper, jnp.concatenate([im, -re], axis=1)], axis=0)

    def stage(re, im, contract):
        def dot(a, b):
            return lax.dot_general(
                a, b, (((1,), (contract,)), ((), ())), preferred_element_type=jnp.float32
            )

        re_hi, re_lo = split_bf16(re)
        im_hi, im_lo = split_bf16(im)
        hi, lo = blocks(re_hi, im_hi), blocks(re_lo, im_lo)
        return dot(hi_ref[...], hi) + (dot(hi_ref[...], lo) + dot(lo_ref[...], hi))

    first = stage(part(0), part(1), 0)
    re, im = first[:, :N1], first[:, N1:]
    turn_re, turn_im = turn_ref[0], turn_ref[1]
    final = stage(re * turn_re - im * turn_im, re * turn_im + im * turn_re, 1)
    for c in range(2):
        for h in range(2):
            start = c * N1 + h * LANES
            out_ref[:, c, h] = final[:, start : start + LANES].reshape(ROWS, 8, LANES)


def core_parity():
    return lax.axis_index("col") % 2


def border_kernel(own_ref, first_ref, second_ref):
    def put(last_ref, initial_ref):
        last_ref[...] = own_ref[ROWS - HALO :]
        initial_ref[...] = own_ref[:HALO]

    parity = core_parity()
    pl.when(parity == 0)(lambda: put(first_ref, second_ref))
    pl.when(parity == 1)(lambda: put(second_ref, first_ref))


def turn_kernel(sources_ref, taps_ref, jac_ref, phase_ref, own_ref, cos_ref, sin_ref, base_ref, weight_ref):
    for tile in range(TILES):
        columns = slice(tile * LANES, (tile + 1) * LANES)
        sine, cosine = sine_cosine(phase_ref[:, columns])
        jac = jac_ref[:, columns]
        cos_ref[:, columns] = jac * cosine
        sin_ref[:, columns] = jac * sine
    shift = HALO - lax.axis_index("row") * ROWS
    for r in range(ROWS):
        base_ref[r : r + 1, :] = jnp.full((1, LANES), sources_ref[0, r] + shift, jnp.int32)
        for j in range(4):
            weight_ref[4 * r + j : 4 * r + j + 1, :] = jnp.full(
                (1, LANES), taps_ref[j, r], jnp.float32
            )


def tilt_kernel(base_ref, weight_ref, own_ref, first_ref, second_ref, cos_ref, sin_ref, out_ref, ext, total, held, sems):
    def put(low_ref, high_ref):
        ext[:HALO] = low_ref[...]
        ext[HALO + ROWS :] = high_ref[...]

    parity = core_parity()
    pl.when(parity == 0)(lambda: put(first_ref, second_ref))
    pl.when(parity == 1)(lambda: put(second_ref, first_ref))
    ext[HALO : HALO + ROWS] = own_ref[...]
    copies = []
    for group in range(GROUPS):
        for r in range(8 * group, 8 * group + 8):
            base = base_ref[r : r + 1, 0:1][0, 0]
            acc = weight_ref[4 * r : 4 * r + 1, :] * ext[base]
            for j in range(1, 4):
                acc = acc + weight_ref[4 * r + j : 4 * r + j + 1, :] * ext[base + j]
            total[r * SLAB : (r + 1) * SLAB, :] = acc
        rows = slice(8 * group, 8 * group + 8)
        for tile in range(TILES):
            columns = slice(tile * LANES, (tile + 1) * LANES)
            start = 8 * group * SLAB + tile_start(tile)
            re = total[pl.ds(start, 8, stride=SLAB), :]
            im = total[pl.ds(16 + start, 8, stride=SLAB), :]
            cosine, sine = cos_ref[rows, columns], sin_ref[rows, columns]
            held[group, 0, :, columns] = re * cosine - im * sine
            held[group, 1, :, columns] = re * sine + im * cosine
        copies.append(
            pltpu.make_async_copy(held.at[group], out_ref.at[:, rows], sems.at[group])
        )
        copies[-1].start()
    for copy in copies:
        copy.wait()


def plane_shift(value, even_step):
    planes, columns = lax.axis_size("row"), lax.axis_size("col")
    pairs = []
    for g in range(planes):
        for c in range(columns):
            to = g + (even_step if c % 2 == 0 else -even_step)
            if 0 <= to < planes:
                pairs.append((g * columns + c, to * columns + c))
    return lax.ppermute(value, ("row", "col"), pairs)


def shards(band, sources, taps, jacobian, phase):
    hi, lo, turn = dft_tables()
    f32 = jnp.float32
    vmem = pl.BlockSpec(memory_space=pltpu.VMEM)
    smem = pl.BlockSpec(memory_space=pltpu.SMEM)
    hbm = pl.BlockSpec(memory_space=pltpu.HBM)
    limit = pltpu.CompilerParams(vmem_limit_bytes=16 * 2**20)
    slabs = pl.pallas_call(
        slab_kernel,
        out_shape=jax.ShapeDtypeStruct((ROWS * SLAB, LANES), f32),
        name="slabs",
        compiler_params=limit,
    )(band)
    rows = lax.all_to_all(
        slabs.reshape(ROWS, 2, 2, 8, LANES), "col", split_axis=0, concat_axis=0, tiled=True
    )
    spectra = pl.pallas_call(
        transform_kernel,
        out_shape=jax.ShapeDtypeStruct((ROWS, 2, 2, 8, LANES), f32),
        name="transform",
        compiler_params=limit,
    )(rows, jnp.asarray(hi), jnp.asarray(lo), jnp.asarray(turn))
    own = lax.all_to_all(spectra, "col", split_axis=0, concat_axis=0, tiled=True)
    own = own.reshape(ROWS, SLAB, LANES)
    border = jax.ShapeDtypeStruct((HALO, SLAB, LANES), f32)
    first, second = pl.pallas_call(
        border_kernel, out_shape=[border, border], name="border_rows", compiler_params=limit
    )(own)
    first = plane_shift(first, 1)
    second = plane_shift(second, -1)
    weights = jax.ShapeDtypeStruct(jacobian.shape, f32)
    cosine, sine, base, weight = pl.pallas_call(
        turn_kernel,
        out_shape=[
            weights,
            weights,
            jax.ShapeDtypeStruct((ROWS, LANES), jnp.int32),
            jax.ShapeDtypeStruct((4 * ROWS, LANES), f32),
        ],
        in_specs=[smem, smem, vmem, vmem, pl.BlockSpec(memory_space=pl.ANY)],
        name="turn",
        compiler_params=limit,
    )(sources.T, taps.T, jacobian, phase, own)
    return pl.pallas_call(
        tilt_kernel,
        out_shape=jax.ShapeDtypeStruct(band.shape, f32),
        in_specs=[vmem] * 7,
        out_specs=hbm,
        scratch_shapes=[
            pltpu.VMEM((ROWS + 2 * HALO, SLAB, LANES), f32),
            pltpu.VMEM((ROWS * SLAB, LANES), f32),
            pltpu.VMEM((GROUPS, 2, 8, TILES * LANES), f32),
            pltpu.SemaphoreType.DMA((GROUPS,)),
        ],
        name="tilt",
        compiler_params=limit,
    )(base, weight, own, first, second, cosine, sine)


def solution(mesh):
    placed = (
        P(None, "row", "col"),
        P("row", None),
        P("row", None),
        P("row", "col"),
        P("row", "col"),
    )
    return jax.shard_map(
        shards, mesh=mesh, in_specs=placed, out_specs=P(None, "row", "col"), check_vma=False
    )
```

```python
import math

import jax
import jax.numpy as jnp
import numpy as np
from jax import lax
from jax.experimental import pallas as pl
from jax.experimental.pallas import tpu as pltpu
from jax.sharding import PartitionSpec as P

N1 = 256
LANES = 128
ROWS = 32
HALO = 16
TILES = 16
HALF_GROUPS = 2
GROUPS = 4
SLAB = 32


def split_bf16(x):
    hi = x.astype(jnp.bfloat16)
    lo = (x - hi.astype(jnp.float32)).astype(jnp.bfloat16)
    return hi, lo


def dft_tables():
    idx = np.arange(N1, dtype=np.int64)
    ang = 2.0 * np.pi * ((idx[:, None] * idx[None, :]) % N1) / N1
    table = np.concatenate([np.cos(ang), np.sin(ang)], axis=1)
    hi = table.astype(np.float32).astype(jnp.bfloat16)
    lo = (table - hi.astype(np.float64)).astype(np.float32).astype(jnp.bfloat16)
    twist = -2.0 * np.pi * (idx[:, None] * idx[None, :]) / (N1 * N1)
    scale = 1.0 / N1
    turn = np.stack([np.cos(twist) * scale, np.sin(twist) * scale]).astype(np.float32)
    return hi, lo, turn


def sine_cosine_coefficients():
    nodes = np.cos((np.arange(400) + 0.5) * np.pi / 400) * (np.pi / 2)
    square = nodes * nodes
    sinc = np.where(nodes == 0, 1.0, np.sin(nodes) / nodes)
    powers = np.stack([square**i for i in range(7)], axis=1)
    sine = np.linalg.lstsq(powers, sinc, rcond=None)[0]
    cosine = np.linalg.lstsq(powers, np.cos(nodes), rcond=None)[0]
    return [float(v) for v in sine], [float(v) for v in cosine]


SINE, COSINE = sine_cosine_coefficients()


def polynomial(square, coefficients):
    total = jnp.full_like(square, coefficients[-1])
    for value in coefficients[-2::-1]:
        total = total * square + value
    return total


def sine_cosine(x):
    half = 0.5 * x
    square = half * half
    s = half * polynomial(square, SINE)
    c = polynomial(square, COSINE)
    return 2.0 * s * c, 1.0 - 2.0 * s * s


def tile_start(tile):
    return (tile % 2) * 8 + tile // 2


def slab_kernel(band_ref, out_ref, held, sems):
    copies = [
        pltpu.make_async_copy(
            band_ref.at[:, 8 * group : 8 * group + 8], held.at[group], sems.at[group]
        )
        for group in range(GROUPS)
    ]
    for copy in copies:
        copy.start()
    for group in range(GROUPS):
        copies[group].wait()
        for c in range(2):
            for tile in range(TILES):
                start = 8 * group * SLAB + c * 16 + tile_start(tile)
                out_ref[pl.ds(start, 8, stride=SLAB), :] = held[
                    group, c, :, tile * LANES : (tile + 1) * LANES
                ]


def transform_kernel(in_ref, hi_ref, lo_ref, turn_ref, out_ref):
    def part(c):
        halves = [in_ref[:, c, h].reshape(N1, LANES) for h in range(2)]
        return jnp.concatenate(halves, axis=1)

    def blocks(re, im):
        upper = jnp.concatenate([re, im], axis=1)
        return jnp.concatenate([upper, jnp.concatenate([im, -re], axis=1)], axis=0)

    def stage(re, im, contract):
        def dot(a, b):
            return lax.dot_general(
                a, b, (((1,), (contract,)), ((), ())), preferred_element_type=jnp.float32
            )

        re_hi, re_lo = split_bf16(re)
        im_hi, im_lo = split_bf16(im)
        hi, lo = blocks(re_hi, im_hi), blocks(re_lo, im_lo)
        return dot(hi_ref[...], hi) + (dot(hi_ref[...], lo) + dot(lo_ref[...], hi))

    first = stage(part(0), part(1), 0)
    re, im = first[:, :N1], first[:, N1:]
    turn_re, turn_im = turn_ref[0], turn_ref[1]
    final = stage(re * turn_re - im * turn_im, re * turn_im + im * turn_re, 1)
    for c in range(2):
        for h in range(2):
            start = c * N1 + h * LANES
            out_ref[:, c, h] = final[:, start : start + LANES].reshape(ROWS, 8, LANES)


def core_parity():
    return lax.axis_index("col") % 2


def border_kernel(own_ref, first_ref, second_ref):
    def put(last_ref, initial_ref):
        last_ref[...] = own_ref[ROWS - HALO :]
        initial_ref[...] = own_ref[:HALO]

    parity = core_parity()
    pl.when(parity == 0)(lambda: put(first_ref, second_ref))
    pl.when(parity == 1)(lambda: put(second_ref, first_ref))


def turn_kernel(sources_ref, taps_ref, jac_ref, phase_ref, own_ref, cos_ref, sin_ref, base_ref, weight_ref):
    for tile in range(TILES):
        columns = slice(tile * LANES, (tile + 1) * LANES)
        sine, cosine = sine_cosine(phase_ref[:, columns])
        jac = jac_ref[:, columns]
        cos_ref[:, columns] = jac * cosine
        sin_ref[:, columns] = jac * sine
    shift = HALO - lax.axis_index("row") * ROWS
    for r in range(ROWS):
        base_ref[r : r + 1, :] = jnp.full((1, LANES), sources_ref[0, r] + shift - (HALO if r >= HALO else 0), jnp.int32)
        for j in range(4):
            weight_ref[4 * r + j : 4 * r + j + 1, :] = jnp.full(
                (1, LANES), taps_ref[j, r], jnp.float32
            )


def tilt_half(late, base_ref, weight_ref, own_ref, halo_ref, cos_ref, sin_ref, out_ref, ext, total, held, sems):
    half = (core_parity() + late) % 2

    @pl.when(half == 0)
    def _():
        ext[:HALO] = halo_ref[...]
        ext[HALO:] = own_ref[...]

    @pl.when(half == 1)
    def _():
        ext[:ROWS] = own_ref[...]
        ext[ROWS:] = halo_ref[...]

    offset = pl.multiple_of(half * HALO, HALO)
    copies = []
    for group in range(HALF_GROUPS):
        for r in range(8 * group, 8 * group + 8):
            base = base_ref[pl.ds(offset + r, 1), 0:1][0, 0]
            weights = weight_ref[pl.ds(pl.multiple_of(4 * offset, 4 * HALO) + 4 * r, 4), :]
            acc = weights[0:1] * ext[base]
            for j in range(1, 4):
                acc = acc + weights[j : j + 1] * ext[base + j]
            total[r * SLAB : (r + 1) * SLAB, :] = acc
        rows = pl.ds(pl.multiple_of(offset + 8 * group, 8), 8)
        for tile in range(TILES):
            columns = slice(tile * LANES, (tile + 1) * LANES)
            start = 8 * group * SLAB + tile_start(tile)
            re = total[pl.ds(start, 8, stride=SLAB), :]
            im = total[pl.ds(16 + start, 8, stride=SLAB), :]
            cosine, sine = cos_ref[rows, columns], sin_ref[rows, columns]
            held[group, 0, :, columns] = re * cosine - im * sine
            held[group, 1, :, columns] = re * sine + im * cosine
        copies.append(
            pltpu.make_async_copy(held.at[group], out_ref.at[:, rows], sems.at[group])
        )
        copies[-1].start()
    for copy in copies:
        copy.wait()


def early_kernel(*refs):
    tilt_half(0, *refs)


def late_kernel(early_ref, *refs):
    tilt_half(1, *refs)


def plane_shift(value, even_step):
    planes, columns = lax.axis_size("row"), lax.axis_size("col")
    pairs = []
    for g in range(planes):
        for c in range(columns):
            to = g + (even_step if c % 2 == 0 else -even_step)
            if 0 <= to < planes:
                pairs.append((g * columns + c, to * columns + c))
    return lax.ppermute(value, ("row", "col"), pairs)


def shards(band, sources, taps, jacobian, phase):
    hi, lo, turn = dft_tables()
    f32 = jnp.float32
    vmem = pl.BlockSpec(memory_space=pltpu.VMEM)
    smem = pl.BlockSpec(memory_space=pltpu.SMEM)
    hbm = pl.BlockSpec(memory_space=pltpu.HBM)
    limit = pltpu.CompilerParams(vmem_limit_bytes=16 * 2**20)
    slabs = pl.pallas_call(
        slab_kernel,
        out_shape=jax.ShapeDtypeStruct((ROWS * SLAB, LANES), f32),
        in_specs=[pl.BlockSpec(memory_space=pl.ANY)],
        scratch_shapes=[
            pltpu.VMEM((GROUPS, 2, 8, TILES * LANES), f32),
            pltpu.SemaphoreType.DMA((GROUPS,)),
        ],
        name="slabs",
        compiler_params=pltpu.CompilerParams(vmem_limit_bytes=56000000),
    )(band)
    rows = lax.all_to_all(
        slabs.reshape(ROWS, 2, 2, 8, LANES), "col", split_axis=0, concat_axis=0, tiled=True
    )
    spectra = pl.pallas_call(
        transform_kernel,
        out_shape=jax.ShapeDtypeStruct((ROWS, 2, 2, 8, LANES), f32),
        name="transform",
        compiler_params=limit,
    )(rows, jnp.asarray(hi), jnp.asarray(lo), jnp.asarray(turn))
    own = lax.all_to_all(spectra, "col", split_axis=0, concat_axis=0, tiled=True)
    own = own.reshape(ROWS, SLAB, LANES)
    border = jax.ShapeDtypeStruct((HALO, SLAB, LANES), f32)
    first, second = pl.pallas_call(
        border_kernel, out_shape=[border, border], name="border_rows", compiler_params=limit
    )(own)
    first = plane_shift(first, 1)
    second = plane_shift(second, -1)
    weights = jax.ShapeDtypeStruct(jacobian.shape, f32)
    cosine, sine, base, weight = pl.pallas_call(
        turn_kernel,
        out_shape=[
            weights,
            weights,
            jax.ShapeDtypeStruct((ROWS, LANES), jnp.int32),
            jax.ShapeDtypeStruct((4 * ROWS, LANES), f32),
        ],
        in_specs=[smem, smem, vmem, vmem, pl.BlockSpec(memory_space=pl.ANY)],
        name="turn",
        compiler_params=limit,
    )(sources.T, taps.T, jacobian, phase, own)
    any_space = pl.BlockSpec(memory_space=pl.ANY)
    scratch = [
        pltpu.VMEM((ROWS + HALO, SLAB, LANES), f32),
        pltpu.VMEM((HALO * SLAB, LANES), f32),
        pltpu.VMEM((HALF_GROUPS, 2, 8, TILES * LANES), f32),
        pltpu.SemaphoreType.DMA((HALF_GROUPS,)),
    ]
    early = pl.pallas_call(
        early_kernel,
        out_shape=jax.ShapeDtypeStruct(band.shape, f32),
        in_specs=[vmem] * 6,
        out_specs=hbm,
        scratch_shapes=scratch,
        name="tilt_early",
        compiler_params=limit,
    )(base, weight, own, first, cosine, sine)
    return pl.pallas_call(
        late_kernel,
        out_shape=jax.ShapeDtypeStruct(band.shape, f32),
        in_specs=[any_space] + [vmem] * 6,
        out_specs=hbm,
        input_output_aliases={0: 0},
        scratch_shapes=scratch,
        name="tilt_late",
        compiler_params=limit,
    )(early, base, weight, own, second, cosine, sine)


def solution(mesh):
    placed = (
        P(None, "row", "col"),
        P("row", None),
        P("row", None),
        P("row", "col"),
        P("row", "col"),
    )
    return jax.shard_map(
        shards, mesh=mesh, in_specs=placed, out_specs=P(None, "row", "col"), check_vma=False
    )
```

```python
import math

import jax
import jax.numpy as jnp
import numpy as np
from jax import lax
from jax.experimental import pallas as pl
from jax.experimental.pallas import tpu as pltpu
from jax.sharding import PartitionSpec as P

N1 = 256
LANES = 128
ROWS = 32
HALO = 16
TILES = 16
HALF_GROUPS = 2
GROUPS = 4
SLAB = 32


def split_bf16(x):
    hi = x.astype(jnp.bfloat16)
    lo = (x - hi.astype(jnp.float32)).astype(jnp.bfloat16)
    return hi, lo


def dft_tables():
    idx = np.arange(N1, dtype=np.int64)
    ang = 2.0 * np.pi * ((idx[:, None] * idx[None, :]) % N1) / N1
    table = np.concatenate([np.cos(ang), np.sin(ang)], axis=1)
    hi = table.astype(np.float32).astype(jnp.bfloat16)
    lo = (table - hi.astype(np.float64)).astype(np.float32).astype(jnp.bfloat16)
    twist = -2.0 * np.pi * (idx[:, None] * idx[None, :]) / (N1 * N1)
    scale = 1.0 / N1
    turn = np.stack([np.cos(twist) * scale, np.sin(twist) * scale]).astype(np.float32)
    return hi, lo, turn


def sine_cosine_coefficients():
    nodes = np.cos((np.arange(400) + 0.5) * np.pi / 400) * (np.pi / 2)
    square = nodes * nodes
    sinc = np.where(nodes == 0, 1.0, np.sin(nodes) / nodes)
    powers = np.stack([square**i for i in range(7)], axis=1)
    sine = np.linalg.lstsq(powers, sinc, rcond=None)[0]
    cosine = np.linalg.lstsq(powers, np.cos(nodes), rcond=None)[0]
    return [float(v) for v in sine], [float(v) for v in cosine]


SINE, COSINE = sine_cosine_coefficients()


def polynomial(square, coefficients):
    total = jnp.full_like(square, coefficients[-1])
    for value in coefficients[-2::-1]:
        total = total * square + value
    return total


def sine_cosine(x):
    half = 0.5 * x
    square = half * half
    s = half * polynomial(square, SINE)
    c = polynomial(square, COSINE)
    return 2.0 * s * c, 1.0 - 2.0 * s * s


def tile_start(tile):
    return (tile % 2) * 8 + tile // 2


def slab_kernel(band_ref, out_ref, held, sems):
    copies = [
        pltpu.make_async_copy(
            band_ref.at[:, 8 * group : 8 * group + 8], held.at[group], sems.at[group]
        )
        for group in range(GROUPS)
    ]
    for copy in copies:
        copy.start()
    for group in range(GROUPS):
        copies[group].wait()
        for c in range(2):
            for tile in range(TILES):
                start = 8 * group * SLAB + c * 16 + tile_start(tile)
                out_ref[pl.ds(start, 8, stride=SLAB), :] = held[
                    group, c, :, tile * LANES : (tile + 1) * LANES
                ]


def transform_kernel(in_ref, hi_ref, lo_ref, turn_ref, out_ref):
    def part(c):
        halves = [in_ref[:, c, h].reshape(N1, LANES) for h in range(2)]
        return jnp.concatenate(halves, axis=1)

    def blocks(re, im):
        upper = jnp.concatenate([re, im], axis=1)
        return jnp.concatenate([upper, jnp.concatenate([im, -re], axis=1)], axis=0)

    def stage(re, im, contract):
        def dot(a, b):
            return lax.dot_general(
                a, b, (((1,), (contract,)), ((), ())), preferred_element_type=jnp.float32
            )

        re_hi, re_lo = split_bf16(re)
        im_hi, im_lo = split_bf16(im)
        hi, lo = blocks(re_hi, im_hi), blocks(re_lo, im_lo)
        return dot(hi_ref[...], hi) + (dot(hi_ref[...], lo) + dot(lo_ref[...], hi))

    first = stage(part(0), part(1), 0)
    re, im = first[:, :N1], first[:, N1:]
    turn_re, turn_im = turn_ref[0], turn_ref[1]
    final = stage(re * turn_re - im * turn_im, re * turn_im + im * turn_re, 1)
    for c in range(2):
        for h in range(2):
            start = c * N1 + h * LANES
            out_ref[:, c, h] = final[:, start : start + LANES].reshape(ROWS, 8, LANES)


def above_first(plane, core):
    return (plane + core + 1) % 2


def my_above_first():
    return above_first(lax.axis_index("row"), lax.axis_index("col"))


def border_kernel(own_ref, first_ref, second_ref):
    def put(last_ref, initial_ref):
        last_ref[...] = own_ref[ROWS - HALO :]
        initial_ref[...] = own_ref[:HALO]

    above = my_above_first()
    pl.when(above == 1)(lambda: put(first_ref, second_ref))
    pl.when(above == 0)(lambda: put(second_ref, first_ref))


def turn_kernel(sources_ref, taps_ref, jac_ref, phase_ref, own_ref, cos_ref, sin_ref, base_ref, weight_ref):
    for tile in range(TILES):
        columns = slice(tile * LANES, (tile + 1) * LANES)
        sine, cosine = sine_cosine(phase_ref[:, columns])
        jac = jac_ref[:, columns]
        cos_ref[:, columns] = jac * cosine
        sin_ref[:, columns] = jac * sine
    shift = HALO - lax.axis_index("row") * ROWS
    for r in range(ROWS):
        base_ref[r : r + 1, :] = jnp.full((1, LANES), sources_ref[0, r] + shift - (HALO if r >= HALO else 0), jnp.int32)
        for j in range(4):
            weight_ref[4 * r + j : 4 * r + j + 1, :] = jnp.full(
                (1, LANES), taps_ref[j, r], jnp.float32
            )


def tilt_half(late, base_ref, weight_ref, own_ref, halo_ref, cos_ref, sin_ref, out_ref, ext, total, held, sems):
    half = (my_above_first() + late) % 2

    @pl.when(half == 0)
    def _():
        ext[:HALO] = halo_ref[...]
        ext[HALO:] = own_ref[...]

    @pl.when(half == 1)
    def _():
        ext[:ROWS] = own_ref[...]
        ext[ROWS:] = halo_ref[...]

    offset = pl.multiple_of(half * HALO, HALO)
    copies = []
    for group in range(HALF_GROUPS):
        for r in range(8 * group, 8 * group + 8):
            base = base_ref[pl.ds(offset + r, 1), 0:1][0, 0]
            weights = weight_ref[pl.ds(pl.multiple_of(4 * offset, 4 * HALO) + 4 * r, 4), :]
            acc = weights[0:1] * ext[base]
            for j in range(1, 4):
                acc = acc + weights[j : j + 1] * ext[base + j]
            total[r * SLAB : (r + 1) * SLAB, :] = acc
        rows = pl.ds(pl.multiple_of(offset + 8 * group, 8), 8)
        for tile in range(TILES):
            columns = slice(tile * LANES, (tile + 1) * LANES)
            start = 8 * group * SLAB + tile_start(tile)
            re = total[pl.ds(start, 8, stride=SLAB), :]
            im = total[pl.ds(16 + start, 8, stride=SLAB), :]
            cosine, sine = cos_ref[rows, columns], sin_ref[rows, columns]
            held[group, 0, :, columns] = re * cosine - im * sine
            held[group, 1, :, columns] = re * sine + im * cosine
        copies.append(
            pltpu.make_async_copy(held.at[group], out_ref.at[:, rows], sems.at[group])
        )
        copies[-1].start()
    for copy in copies:
        copy.wait()


def early_kernel(*refs):
    tilt_half(0, *refs)


def late_kernel(early_ref, *refs):
    tilt_half(1, *refs)


def swap(value, late):
    planes, columns = lax.axis_size("row"), lax.axis_size("col")
    pairs = []
    for g in range(planes):
        for c in range(columns):
            to = g + (1 if above_first(g, c) != late else -1)
            if 0 <= to < planes:
                pairs.append((g * columns + c, to * columns + c))
    return lax.ppermute(value, ("row", "col"), pairs)


def shards(band, sources, taps, jacobian, phase):
    hi, lo, turn = dft_tables()
    f32 = jnp.float32
    vmem = pl.BlockSpec(memory_space=pltpu.VMEM)
    smem = pl.BlockSpec(memory_space=pltpu.SMEM)
    hbm = pl.BlockSpec(memory_space=pltpu.HBM)
    limit = pltpu.CompilerParams(vmem_limit_bytes=16 * 2**20)
    slabs = pl.pallas_call(
        slab_kernel,
        out_shape=jax.ShapeDtypeStruct((ROWS * SLAB, LANES), f32),
        in_specs=[pl.BlockSpec(memory_space=pl.ANY)],
        scratch_shapes=[
            pltpu.VMEM((GROUPS, 2, 8, TILES * LANES), f32),
            pltpu.SemaphoreType.DMA((GROUPS,)),
        ],
        name="slabs",
        compiler_params=pltpu.CompilerParams(vmem_limit_bytes=56000000),
    )(band)
    rows = lax.all_to_all(
        slabs.reshape(ROWS, 2, 2, 8, LANES), "col", split_axis=0, concat_axis=0, tiled=True
    )
    spectra = pl.pallas_call(
        transform_kernel,
        out_shape=jax.ShapeDtypeStruct((ROWS, 2, 2, 8, LANES), f32),
        name="transform",
        compiler_params=limit,
    )(rows, jnp.asarray(hi), jnp.asarray(lo), jnp.asarray(turn))
    own = lax.all_to_all(spectra, "col", split_axis=0, concat_axis=0, tiled=True)
    own = own.reshape(ROWS, SLAB, LANES)
    border = jax.ShapeDtypeStruct((HALO, SLAB, LANES), f32)
    first, second = pl.pallas_call(
        border_kernel, out_shape=[border, border], name="border_rows", compiler_params=limit
    )(own)
    first = swap(first, 0)
    second = swap(second, 1)
    weights = jax.ShapeDtypeStruct(jacobian.shape, f32)
    cosine, sine, base, weight = pl.pallas_call(
        turn_kernel,
        out_shape=[
            weights,
            weights,
            jax.ShapeDtypeStruct((ROWS, LANES), jnp.int32),
            jax.ShapeDtypeStruct((4 * ROWS, LANES), f32),
        ],
        in_specs=[smem, smem, vmem, vmem, pl.BlockSpec(memory_space=pl.ANY)],
        name="turn",
        compiler_params=limit,
    )(sources.T, taps.T, jacobian, phase, own)
    any_space = pl.BlockSpec(memory_space=pl.ANY)
    scratch = [
        pltpu.VMEM((ROWS + HALO, SLAB, LANES), f32),
        pltpu.VMEM((HALO * SLAB, LANES), f32),
        pltpu.VMEM((HALF_GROUPS, 2, 8, TILES * LANES), f32),
        pltpu.SemaphoreType.DMA((HALF_GROUPS,)),
    ]
    early = pl.pallas_call(
        early_kernel,
        out_shape=jax.ShapeDtypeStruct(band.shape, f32),
        in_specs=[vmem] * 6,
        out_specs=hbm,
        scratch_shapes=scratch,
        name="tilt_early",
        compiler_params=limit,
    )(base, weight, own, first, cosine, sine)
    return pl.pallas_call(
        late_kernel,
        out_shape=jax.ShapeDtypeStruct(band.shape, f32),
        in_specs=[any_space] + [vmem] * 6,
        out_specs=hbm,
        input_output_aliases={0: 0},
        scratch_shapes=scratch,
        name="tilt_late",
        compiler_params=limit,
    )(early, base, weight, own, second, cosine, sine)


def solution(mesh):
    placed = (
        P(None, "row", "col"),
        P("row", None),
        P("row", None),
        P("row", "col"),
        P("row", "col"),
    )
    return jax.shard_map(
        shards, mesh=mesh, in_specs=placed, out_specs=P(None, "row", "col"), check_vma=False
    )
```

```python
import math

import jax
import jax.numpy as jnp
import numpy as np
from jax import lax
from jax.experimental import pallas as pl
from jax.experimental.pallas import tpu as pltpu
from jax.sharding import PartitionSpec as P

N1 = 256
LANES = 128
ROWS = 32
HALO = 16
TILES = 16
HALF_GROUPS = 2
GROUPS = 4
SLAB = 32


def split_bf16(x):
    hi = x.astype(jnp.bfloat16)
    lo = (x - hi.astype(jnp.float32)).astype(jnp.bfloat16)
    return hi, lo


def dft_tables():
    idx = np.arange(N1, dtype=np.int64)
    ang = 2.0 * np.pi * ((idx[:, None] * idx[None, :]) % N1) / N1
    table = np.concatenate([np.cos(ang), np.sin(ang)], axis=1)
    hi = table.astype(np.float32).astype(jnp.bfloat16)
    lo = (table - hi.astype(np.float64)).astype(np.float32).astype(jnp.bfloat16)
    twist = -2.0 * np.pi * (idx[:, None] * idx[None, :]) / (N1 * N1)
    scale = 1.0 / N1
    turn = np.stack([np.cos(twist) * scale, np.sin(twist) * scale]).astype(np.float32)
    return hi, lo, turn


def sine_cosine_coefficients():
    nodes = np.cos((np.arange(400) + 0.5) * np.pi / 400) * (np.pi / 2)
    square = nodes * nodes
    sinc = np.where(nodes == 0, 1.0, np.sin(nodes) / nodes)
    powers = np.stack([square**i for i in range(7)], axis=1)
    sine = np.linalg.lstsq(powers, sinc, rcond=None)[0]
    cosine = np.linalg.lstsq(powers, np.cos(nodes), rcond=None)[0]
    return [float(v) for v in sine], [float(v) for v in cosine]


SINE, COSINE = sine_cosine_coefficients()


def polynomial(square, coefficients):
    total = jnp.full_like(square, coefficients[-1])
    for value in coefficients[-2::-1]:
        total = total * square + value
    return total


def sine_cosine(x):
    half = 0.5 * x
    square = half * half
    s = half * polynomial(square, SINE)
    c = polynomial(square, COSINE)
    return 2.0 * s * c, 1.0 - 2.0 * s * s


def tile_start(tile):
    return (tile % 2) * 8 + tile // 2


def slab_kernel(band_ref, out_ref, held, sems):
    copies = [
        pltpu.make_async_copy(
            band_ref.at[:, 8 * group : 8 * group + 8], held.at[group], sems.at[group]
        )
        for group in range(GROUPS)
    ]
    for copy in copies:
        copy.start()
    for group in range(GROUPS):
        copies[group].wait()
        for c in range(2):
            for tile in range(TILES):
                start = 8 * group * SLAB + c * 16 + tile_start(tile)
                out_ref[pl.ds(start, 8, stride=SLAB), :] = held[
                    group, c, :, tile * LANES : (tile + 1) * LANES
                ]


def transform_kernel(in_ref, hi_ref, lo_ref, turn_ref, out_ref):
    def part(c):
        halves = [in_ref[:, c, h].reshape(N1, LANES) for h in range(2)]
        return jnp.concatenate(halves, axis=1)

    def blocks(re, im):
        upper = jnp.concatenate([re, im], axis=1)
        return jnp.concatenate([upper, jnp.concatenate([im, -re], axis=1)], axis=0)

    def stage(re, im, contract):
        def dot(a, b):
            return lax.dot_general(
                a, b, (((1,), (contract,)), ((), ())), preferred_element_type=jnp.float32
            )

        re_hi, re_lo = split_bf16(re)
        im_hi, im_lo = split_bf16(im)
        hi, lo = blocks(re_hi, im_hi), blocks(re_lo, im_lo)
        return dot(hi_ref[...], hi) + (dot(hi_ref[...], lo) + dot(lo_ref[...], hi))

    first = stage(part(0), part(1), 0)
    re, im = first[:, :N1], first[:, N1:]
    turn_re, turn_im = turn_ref[0], turn_ref[1]
    final = stage(re * turn_re - im * turn_im, re * turn_im + im * turn_re, 1)
    for c in range(2):
        for h in range(2):
            start = c * N1 + h * LANES
            out_ref[:, c, h] = final[:, start : start + LANES].reshape(ROWS, 8, LANES)


def above_first(plane, core):
    return (plane + core + 1) % 2


def my_above_first():
    return above_first(lax.axis_index("row"), lax.axis_index("col"))


def border_kernel(own_ref, first_ref, second_ref):
    def put(last_ref, initial_ref):
        last_ref[...] = own_ref[ROWS - HALO :]
        initial_ref[...] = own_ref[:HALO]

    above = my_above_first()
    pl.when(above == 1)(lambda: put(first_ref, second_ref))
    pl.when(above == 0)(lambda: put(second_ref, first_ref))


def turn_kernel(sources_ref, taps_ref, jac_ref, phase_ref, own_ref, cos_ref, sin_ref, base_ref, weight_ref):
    for tile in range(TILES):
        columns = slice(tile * LANES, (tile + 1) * LANES)
        sine, cosine = sine_cosine(phase_ref[:, columns])
        jac = jac_ref[:, columns]
        cos_ref[:, columns] = jac * cosine
        sin_ref[:, columns] = jac * sine
    shift = HALO - lax.axis_index("row") * ROWS
    for r in range(ROWS):
        base_ref[r : r + 1, :] = jnp.full((1, LANES), sources_ref[0, r] + shift - (HALO if r >= HALO else 0), jnp.int32)
        for j in range(4):
            weight_ref[4 * r + j : 4 * r + j + 1, :] = jnp.full(
                (1, LANES), taps_ref[j, r], jnp.float32
            )


def turn_out(group, offset, total, cos_ref, sin_ref, held, out_ref, sems):
    rows = pl.ds(pl.multiple_of(offset + 8 * group, 8), 8)
    for tile in range(TILES):
        columns = slice(tile * LANES, (tile + 1) * LANES)
        start = 8 * group * SLAB + tile_start(tile)
        re = total[pl.ds(start, 8, stride=SLAB), :]
        im = total[pl.ds(16 + start, 8, stride=SLAB), :]
        cosine, sine = cos_ref[rows, columns], sin_ref[rows, columns]
        held[group, 0, :, columns] = re * cosine - im * sine
        held[group, 1, :, columns] = re * sine + im * cosine
    copy = pltpu.make_async_copy(held.at[group], out_ref.at[:, rows], sems.at[group])
    copy.start()
    return copy


def row_terms(base_ref, weight_ref, offset, r):
    base = base_ref[pl.ds(offset + r, 1), :]
    weights = weight_ref[pl.ds(pl.multiple_of(4 * offset, 4 * HALO) + 4 * r, 4), :]
    return base, base[0:1, 0:1][0, 0], weights


def early_kernel(base_ref, weight_ref, own_ref, halo_ref, cos_ref, sin_ref, out_ref, part_ref, ext, total, held, sems):
    half = my_above_first()

    @pl.when(half == 0)
    def _():
        ext[:HALO] = halo_ref[...]
        ext[HALO:] = own_ref[...]

    @pl.when(half == 1)
    def _():
        ext[:ROWS] = own_ref[...]
        ext[ROWS:] = halo_ref[...]

    offset = pl.multiple_of(half * HALO, HALO)
    copies = []
    for group in range(HALF_GROUPS):
        for r in range(8 * group, 8 * group + 8):
            _, base, weights = row_terms(base_ref, weight_ref, offset, r)
            acc = weights[0:1] * ext[base]
            for j in range(1, 4):
                acc = acc + weights[j : j + 1] * ext[base + j]
            total[r * SLAB : (r + 1) * SLAB, :] = acc
        copies.append(turn_out(group, offset, total, cos_ref, sin_ref, held, out_ref, sems))
    other = 1 - half
    first_own = HALO * (1 - other)
    offset = pl.multiple_of(other * HALO, HALO)
    for r in range(HALO):
        rows, base, weights = row_terms(base_ref, weight_ref, offset, r)
        acc = jnp.zeros((SLAB, LANES), jnp.float32)
        for j in range(4):
            place = rows + (j - first_own)
            inside = jnp.logical_and(place >= 0, place < ROWS)
            tap = jnp.where(inside, weights[j : j + 1], 0.0)
            acc = acc + tap * own_ref[jnp.clip(base + j - first_own, 0, ROWS - 1)]
        part_ref[r * SLAB : (r + 1) * SLAB, :] = acc
    for copy in copies:
        copy.wait()


def late_kernel(early_ref, base_ref, weight_ref, part_ref, halo_ref, cos_ref, sin_ref, out_ref, total, held, sems):
    half = 1 - my_above_first()
    first_halo = ROWS * half
    offset = pl.multiple_of(half * HALO, HALO)
    copies = []
    for group in range(HALF_GROUPS):
        for r in range(8 * group, 8 * group + 8):
            rows, base, weights = row_terms(base_ref, weight_ref, offset, r)
            acc = part_ref[r * SLAB : (r + 1) * SLAB, :]
            for j in range(4):
                place = rows + (j - first_halo)
                inside = jnp.logical_and(place >= 0, place < HALO)
                tap = jnp.where(inside, weights[j : j + 1], 0.0)
                acc = acc + tap * halo_ref[jnp.clip(base + j - first_halo, 0, HALO - 1)]
            total[r * SLAB : (r + 1) * SLAB, :] = acc
        copies.append(turn_out(group, offset, total, cos_ref, sin_ref, held, out_ref, sems))
    for copy in copies:
        copy.wait()


def swap(value, late):
    planes, columns = lax.axis_size("row"), lax.axis_size("col")
    pairs = []
    for g in range(planes):
        for c in range(columns):
            to = g + (1 if above_first(g, c) != late else -1)
            if 0 <= to < planes:
                pairs.append((g * columns + c, to * columns + c))
    return lax.ppermute(value, ("row", "col"), pairs)


def shards(band, sources, taps, jacobian, phase):
    hi, lo, turn = dft_tables()
    f32 = jnp.float32
    vmem = pl.BlockSpec(memory_space=pltpu.VMEM)
    smem = pl.BlockSpec(memory_space=pltpu.SMEM)
    hbm = pl.BlockSpec(memory_space=pltpu.HBM)
    limit = pltpu.CompilerParams(vmem_limit_bytes=16 * 2**20)
    slabs = pl.pallas_call(
        slab_kernel,
        out_shape=jax.ShapeDtypeStruct((ROWS * SLAB, LANES), f32),
        in_specs=[pl.BlockSpec(memory_space=pl.ANY)],
        scratch_shapes=[
            pltpu.VMEM((GROUPS, 2, 8, TILES * LANES), f32),
            pltpu.SemaphoreType.DMA((GROUPS,)),
        ],
        name="slabs",
        compiler_params=pltpu.CompilerParams(vmem_limit_bytes=56000000),
    )(band)
    rows = lax.all_to_all(
        slabs.reshape(ROWS, 2, 2, 8, LANES), "col", split_axis=0, concat_axis=0, tiled=True
    )
    spectra = pl.pallas_call(
        transform_kernel,
        out_shape=jax.ShapeDtypeStruct((ROWS, 2, 2, 8, LANES), f32),
        name="transform",
        compiler_params=limit,
    )(rows, jnp.asarray(hi), jnp.asarray(lo), jnp.asarray(turn))
    own = lax.all_to_all(spectra, "col", split_axis=0, concat_axis=0, tiled=True)
    own = own.reshape(ROWS, SLAB, LANES)
    border = jax.ShapeDtypeStruct((HALO, SLAB, LANES), f32)
    first, second = pl.pallas_call(
        border_kernel, out_shape=[border, border], name="border_rows", compiler_params=limit
    )(own)
    first = swap(first, 0)
    second = swap(second, 1)
    weights = jax.ShapeDtypeStruct(jacobian.shape, f32)
    cosine, sine, base, weight = pl.pallas_call(
        turn_kernel,
        out_shape=[
            weights,
            weights,
            jax.ShapeDtypeStruct((ROWS, LANES), jnp.int32),
            jax.ShapeDtypeStruct((4 * ROWS, LANES), f32),
        ],
        in_specs=[smem, smem, vmem, vmem, pl.BlockSpec(memory_space=pl.ANY)],
        name="turn",
        compiler_params=limit,
    )(sources.T, taps.T, jacobian, phase, own)
    any_space = pl.BlockSpec(memory_space=pl.ANY)
    scratch = [
        pltpu.VMEM((HALO * SLAB, LANES), f32),
        pltpu.VMEM((HALF_GROUPS, 2, 8, TILES * LANES), f32),
        pltpu.SemaphoreType.DMA((HALF_GROUPS,)),
    ]
    early, part = pl.pallas_call(
        early_kernel,
        out_shape=[
            jax.ShapeDtypeStruct(band.shape, f32),
            jax.ShapeDtypeStruct((HALO * SLAB, LANES), f32),
        ],
        in_specs=[vmem] * 6,
        out_specs=[hbm, vmem],
        scratch_shapes=[pltpu.VMEM((ROWS + HALO, SLAB, LANES), f32)] + scratch,
        name="tilt_early",
        compiler_params=limit,
    )(base, weight, own, first, cosine, sine)
    return pl.pallas_call(
        late_kernel,
        out_shape=jax.ShapeDtypeStruct(band.shape, f32),
        in_specs=[any_space] + [vmem] * 6,
        out_specs=hbm,
        input_output_aliases={0: 0},
        scratch_shapes=scratch,
        name="tilt_late",
        compiler_params=limit,
    )(early, base, weight, part, second, cosine, sine)


def solution(mesh):
    placed = (
        P(None, "row", "col"),
        P("row", None),
        P("row", None),
        P("row", "col"),
        P("row", "col"),
    )
    return jax.shard_map(
        shards, mesh=mesh, in_specs=placed, out_specs=P(None, "row", "col"), check_vma=False
    )
```

```python
import math

import jax
import jax.numpy as jnp
import numpy as np
from jax import lax
from jax.experimental import pallas as pl
from jax.experimental.pallas import tpu as pltpu
from jax.sharding import PartitionSpec as P

N1 = 256
LANES = 128
ROWS = 32
HALO = 16
PIECE = 8
TILES = 16
HALF_GROUPS = 2
GROUPS = 4
SLAB = 32


def split_bf16(x):
    hi = x.astype(jnp.bfloat16)
    lo = (x - hi.astype(jnp.float32)).astype(jnp.bfloat16)
    return hi, lo


def dft_tables():
    idx = np.arange(N1, dtype=np.int64)
    ang = 2.0 * np.pi * ((idx[:, None] * idx[None, :]) % N1) / N1
    table = np.concatenate([np.cos(ang), np.sin(ang)], axis=1)
    hi = table.astype(np.float32).astype(jnp.bfloat16)
    lo = (table - hi.astype(np.float64)).astype(np.float32).astype(jnp.bfloat16)
    twist = -2.0 * np.pi * (idx[:, None] * idx[None, :]) / (N1 * N1)
    scale = 1.0 / N1
    turn = np.stack([np.cos(twist) * scale, np.sin(twist) * scale]).astype(np.float32)
    return hi, lo, turn


def sine_cosine_coefficients():
    nodes = np.cos((np.arange(400) + 0.5) * np.pi / 400) * (np.pi / 2)
    square = nodes * nodes
    sinc = np.where(nodes == 0, 1.0, np.sin(nodes) / nodes)
    powers = np.stack([square**i for i in range(7)], axis=1)
    sine = np.linalg.lstsq(powers, sinc, rcond=None)[0]
    cosine = np.linalg.lstsq(powers, np.cos(nodes), rcond=None)[0]
    return [float(v) for v in sine], [float(v) for v in cosine]


SINE, COSINE = sine_cosine_coefficients()


def polynomial(square, coefficients):
    total = jnp.full_like(square, coefficients[-1])
    for value in coefficients[-2::-1]:
        total = total * square + value
    return total


def sine_cosine(x):
    half = 0.5 * x
    square = half * half
    s = half * polynomial(square, SINE)
    c = polynomial(square, COSINE)
    return 2.0 * s * c, 1.0 - 2.0 * s * s


def tile_start(tile):
    return (tile % 2) * 8 + tile // 2


def slab_kernel(band_ref, out_ref, held, sems):
    copies = [
        pltpu.make_async_copy(
            band_ref.at[:, 8 * group : 8 * group + 8], held.at[group], sems.at[group]
        )
        for group in range(GROUPS)
    ]
    for copy in copies:
        copy.start()
    for group in range(GROUPS):
        copies[group].wait()
        for c in range(2):
            for tile in range(TILES):
                start = 8 * group * SLAB + c * 16 + tile_start(tile)
                out_ref[pl.ds(start, 8, stride=SLAB), :] = held[
                    group, c, :, tile * LANES : (tile + 1) * LANES
                ]


def transform_kernel(in_ref, hi_ref, lo_ref, turn_ref, out_ref):
    def part(c):
        halves = [in_ref[:, c, h].reshape(N1, LANES) for h in range(2)]
        return jnp.concatenate(halves, axis=1)

    def blocks(re, im):
        upper = jnp.concatenate([re, im], axis=1)
        return jnp.concatenate([upper, jnp.concatenate([im, -re], axis=1)], axis=0)

    def stage(re, im, contract):
        def dot(a, b):
            return lax.dot_general(
                a, b, (((1,), (contract,)), ((), ())), preferred_element_type=jnp.float32
            )

        re_hi, re_lo = split_bf16(re)
        im_hi, im_lo = split_bf16(im)
        hi, lo = blocks(re_hi, im_hi), blocks(re_lo, im_lo)
        return dot(hi_ref[...], hi) + (dot(hi_ref[...], lo) + dot(lo_ref[...], hi))

    first = stage(part(0), part(1), 0)
    re, im = first[:, :N1], first[:, N1:]
    turn_re, turn_im = turn_ref[0], turn_ref[1]
    final = stage(re * turn_re - im * turn_im, re * turn_im + im * turn_re, 1)
    for c in range(2):
        for h in range(2):
            start = c * N1 + h * LANES
            out_ref[:, c, h] = final[:, start : start + LANES].reshape(ROWS, 8, LANES)


def above_first(plane, core):
    return (plane + core + 1) % 2


def my_above_first():
    return above_first(lax.axis_index("row"), lax.axis_index("col"))


def border_kernel(own_ref, first_ref, second_ref):
    def put(last_ref, initial_ref):
        last_ref[...] = own_ref[ROWS - HALO :]
        initial_ref[...] = own_ref[:HALO]

    above = my_above_first()
    pl.when(above == 1)(lambda: put(first_ref, second_ref))
    pl.when(above == 0)(lambda: put(second_ref, first_ref))


def turn_kernel(sources_ref, taps_ref, jac_ref, phase_ref, own_ref, cos_ref, sin_ref, base_ref, weight_ref):
    for tile in range(TILES):
        columns = slice(tile * LANES, (tile + 1) * LANES)
        sine, cosine = sine_cosine(phase_ref[:, columns])
        jac = jac_ref[:, columns]
        cos_ref[:, columns] = jac * cosine
        sin_ref[:, columns] = jac * sine
    shift = HALO - lax.axis_index("row") * ROWS
    for r in range(ROWS):
        base_ref[r : r + 1, :] = jnp.full((1, LANES), sources_ref[0, r] + shift - (HALO if r >= HALO else 0), jnp.int32)
        for j in range(4):
            weight_ref[4 * r + j : 4 * r + j + 1, :] = jnp.full(
                (1, LANES), taps_ref[j, r], jnp.float32
            )


def tilt_half(late, base_ref, weight_ref, own_ref, halo_ref, cos_ref, sin_ref, out_ref, ext, total, held, sems):
    half = (my_above_first() + late) % 2

    @pl.when(half == 0)
    def _():
        ext[:HALO] = halo_ref[...]
        ext[HALO:] = own_ref[...]

    @pl.when(half == 1)
    def _():
        ext[:ROWS] = own_ref[...]
        ext[ROWS:] = halo_ref[...]

    offset = pl.multiple_of(half * HALO, HALO)
    copies = []
    for group in range(HALF_GROUPS):
        for r in range(8 * group, 8 * group + 8):
            base = base_ref[pl.ds(offset + r, 1), 0:1][0, 0]
            weights = weight_ref[pl.ds(pl.multiple_of(4 * offset, 4 * HALO) + 4 * r, 4), :]
            acc = weights[0:1] * ext[base]
            for j in range(1, 4):
                acc = acc + weights[j : j + 1] * ext[base + j]
            total[r * SLAB : (r + 1) * SLAB, :] = acc
        rows = pl.ds(pl.multiple_of(offset + 8 * group, 8), 8)
        for tile in range(TILES):
            columns = slice(tile * LANES, (tile + 1) * LANES)
            start = 8 * group * SLAB + tile_start(tile)
            re = total[pl.ds(start, 8, stride=SLAB), :]
            im = total[pl.ds(16 + start, 8, stride=SLAB), :]
            cosine, sine = cos_ref[rows, columns], sin_ref[rows, columns]
            held[group, 0, :, columns] = re * cosine - im * sine
            held[group, 1, :, columns] = re * sine + im * cosine
            if tile % PIECE == PIECE - 1:
                piece = slice((tile + 1 - PIECE) * LANES, (tile + 1) * LANES)
                copies.append(
                    pltpu.make_async_copy(
                        held.at[group, :, :, piece],
                        out_ref.at[:, rows, piece],
                        sems.at[len(copies)],
                    )
                )
                copies[-1].start()
    for copy in copies:
        copy.wait()


def early_kernel(*refs):
    tilt_half(0, *refs)


def late_kernel(early_ref, *refs):
    tilt_half(1, *refs)


def swap(value, late):
    planes, columns = lax.axis_size("row"), lax.axis_size("col")
    pairs = []
    for g in range(planes):
        for c in range(columns):
            to = g + (1 if above_first(g, c) != late else -1)
            if 0 <= to < planes:
                pairs.append((g * columns + c, to * columns + c))
    return lax.ppermute(value, ("row", "col"), pairs)


def shards(band, sources, taps, jacobian, phase):
    hi, lo, turn = dft_tables()
    f32 = jnp.float32
    vmem = pl.BlockSpec(memory_space=pltpu.VMEM)
    smem = pl.BlockSpec(memory_space=pltpu.SMEM)
    hbm = pl.BlockSpec(memory_space=pltpu.HBM)
    limit = pltpu.CompilerParams(vmem_limit_bytes=16 * 2**20)
    slabs = pl.pallas_call(
        slab_kernel,
        out_shape=jax.ShapeDtypeStruct((ROWS * SLAB, LANES), f32),
        in_specs=[pl.BlockSpec(memory_space=pl.ANY)],
        scratch_shapes=[
            pltpu.VMEM((GROUPS, 2, 8, TILES * LANES), f32),
            pltpu.SemaphoreType.DMA((GROUPS,)),
        ],
        name="slabs",
        compiler_params=pltpu.CompilerParams(vmem_limit_bytes=56000000),
    )(band)
    rows = lax.all_to_all(
        slabs.reshape(ROWS, 2, 2, 8, LANES), "col", split_axis=0, concat_axis=0, tiled=True
    )
    spectra = pl.pallas_call(
        transform_kernel,
        out_shape=jax.ShapeDtypeStruct((ROWS, 2, 2, 8, LANES), f32),
        name="transform",
        compiler_params=limit,
    )(rows, jnp.asarray(hi), jnp.asarray(lo), jnp.asarray(turn))
    own = lax.all_to_all(spectra, "col", split_axis=0, concat_axis=0, tiled=True)
    own = own.reshape(ROWS, SLAB, LANES)
    border = jax.ShapeDtypeStruct((HALO, SLAB, LANES), f32)
    first, second = pl.pallas_call(
        border_kernel, out_shape=[border, border], name="border_rows", compiler_params=limit
    )(own)
    first = swap(first, 0)
    second = swap(second, 1)
    weights = jax.ShapeDtypeStruct(jacobian.shape, f32)
    cosine, sine, base, weight = pl.pallas_call(
        turn_kernel,
        out_shape=[
            weights,
            weights,
            jax.ShapeDtypeStruct((ROWS, LANES), jnp.int32),
            jax.ShapeDtypeStruct((4 * ROWS, LANES), f32),
        ],
        in_specs=[smem, smem, vmem, vmem, pl.BlockSpec(memory_space=pl.ANY)],
        name="turn",
        compiler_params=limit,
    )(sources.T, taps.T, jacobian, phase, own)
    any_space = pl.BlockSpec(memory_space=pl.ANY)
    scratch = [
        pltpu.VMEM((ROWS + HALO, SLAB, LANES), f32),
        pltpu.VMEM((HALO * SLAB, LANES), f32),
        pltpu.VMEM((HALF_GROUPS, 2, 8, TILES * LANES), f32),
        pltpu.SemaphoreType.DMA((HALF_GROUPS * TILES // PIECE,)),
    ]
    early = pl.pallas_call(
        early_kernel,
        out_shape=jax.ShapeDtypeStruct(band.shape, f32),
        in_specs=[vmem] * 6,
        out_specs=hbm,
        scratch_shapes=scratch,
        name="tilt_early",
        compiler_params=limit,
    )(base, weight, own, first, cosine, sine)
    return pl.pallas_call(
        late_kernel,
        out_shape=jax.ShapeDtypeStruct(band.shape, f32),
        in_specs=[any_space] + [vmem] * 6,
        out_specs=hbm,
        input_output_aliases={0: 0},
        scratch_shapes=scratch,
        name="tilt_late",
        compiler_params=limit,
    )(early, base, weight, own, second, cosine, sine)


def solution(mesh):
    placed = (
        P(None, "row", "col"),
        P("row", None),
        P("row", None),
        P("row", "col"),
        P("row", "col"),
    )
    return jax.shard_map(
        shards, mesh=mesh, in_specs=placed, out_specs=P(None, "row", "col"), check_vma=False
    )
```
